32 devices in a mesh: groups: 2 (over y), ranks: 8 (over z, x), tp: 2 (over core).
Axes of the slice: x: 2, y: 2, z: 4, core: 2. Of those that a mesh axis runs over, the one named last changes fastest.
Arguments:
- queries: bfloat16 [128, 6144], P(('groups', 'ranks'), 'tp'), parts along dimension 0, may hold values from -8 to 8
- cache_keys: bfloat16 [1024, 16, 1024], P(('groups', 'ranks'), None, 'tp'), parts along dimension 0, may hold values from -1000 to 1000
- cache_values: bfloat16 [1024, 16, 1024], P(('groups', 'ranks'), None, 'tp'), parts along dimension 0, may hold values from -6 to 6
- fresh_keys: bfloat16 [128, 1024], P(('groups', 'ranks'), 'tp'), parts along dimension 0, may hold values from -7 to 7
- fresh_values: bfloat16 [128, 1024], P(('groups', 'ranks'), 'tp'), parts along dimension 0, may hold values from -6 to 6
- block_table: int32 [128, 8], P(('groups', 'ranks')), parts along dimension 0, may hold values from 0 to 63, as said below
- lengths: int32 [128], P(('groups', 'ranks')), parts along dimension 0, may hold values from 16 to 127, as said below
- stream: bfloat16 [128, 6144], P(('groups', 'ranks')), parts along dimension 0, may hold values from -2 to 2
- norm_gain: bfloat16 [6144], replicated, may hold values from 0.099609375 to 1.8984375
- router: bfloat16 [6144, 4], replicated, may hold values from -0.078125 to 0.078125
- routes: int32 [128, 2], P(('groups', 'ranks')), parts along dimension 0, may hold values from 0 to 3, all different within a row; in each aligned block of 8 rows (0 to 7, 8 to 15, ...) at most 6 rows name the same one
- expert_gate: bfloat16 [6144, 32768], P(None, ('ranks', 'tp')), may hold values from -0.078125 to 0.078125
- expert_up: bfloat16 [6144, 32768], P(None, ('ranks', 'tp')), may hold values from -0.078125 to 0.078125
- expert_down: bfloat16 [32768, 6144], P(('ranks', 'tp')), may hold values from -0.0625 to 0.0625
Outputs:
- layer_out: bfloat16 [128, 6144], P(('groups', 'ranks'), 'tp'), parts along dimension 0
- moved_keys: bfloat16 [16, 128, 1024], P(('groups', 'ranks'), None, 'tp'), parts along dimension 0
- moved_values: bfloat16 [16, 128, 1024], P(('groups', 'ranks'), None, 'tp'), parts along dimension 0
The draws below stay inside these ranges and needn't reach their ends.
There are 2 independent parts, one for each index of `groups`. The reference program is written for one: setup_inputs(seed, part) draws one part's arguments, and reference() takes and returns one part's arrays. A program takes and returns all parts, laid end to end along the dimension named above; an argument that names none is the same for every part. Nothing has to cross between parts.
Inputs may be any that keep to these rules, and one draw needn't show every extreme that they name: `block_table`: the rows of each rank form a permutation of 0 to 63. `lengths`: some request has 127.
All inputs are finite; a program needn't handle non-finite values.
Results may differ from the reference program's by a relative error of at most 0.018.
Values may be sent and summed in bfloat16 or wider, within the bound.
A program may use at most 192 MiB of HBM per device.

```python
import math
import jax
import jax.numpy as jnp
import numpy as np
from jax import lax

KVH = 8
HD = 128
D = 6144
EXPERTS = 4
FFW = 8192
TOK_DEV = 8
CAP = 6
CTX = 128
BLK = 16
NBLK = 8
REQS = 64
N_RANKS = 8


def shared_queries(key):
    inner = jax.random.fold_in(key, 101)
    return jnp.clip(jax.random.normal(inner, (REQS, D), jnp.float32), -8.0, 8.0)


def shared_table(key):
    inner = jax.random.fold_in(key, 202)
    rank_count = REQS // TOK_DEV
    keys = jax.random.split(inner, rank_count)
    perms = jax.vmap(lambda each: jax.random.permutation(each, TOK_DEV * NBLK))(keys)
    return perms.reshape(REQS, NBLK).astype(jnp.int32)


def draw_queries(key, part):
    return shared_queries(key).astype(jnp.bfloat16)


def draw_block_table(key, part):
    return shared_table(key)


def draw_lengths(key, part):
    key = jax.random.fold_in(key, 7)
    drawn = jax.random.randint(key, (REQS,), BLK, CTX, dtype=jnp.int32)
    return drawn.at[0].set(CTX - 1)


def draw_cache_keys(key, part):
    key = jax.random.fold_in(key, 5)
    pooled = jnp.clip(1.2 * jax.random.normal(key, (REQS * NBLK, BLK, KVH * HD), jnp.float32), -7.0, 7.0)
    return pooled.astype(jnp.bfloat16)


def steps_of(rng, shape, shards, low, largest):
    factor_of = 1.0
    for axis_at, blocks in shards:
        heights = jax.random.uniform(jax.random.fold_in(jax.random.fold_in(rng, 6), axis_at), (blocks,), jnp.float32, low / len(shards), largest / len(shards))
        factor_of = factor_of * jnp.repeat(jnp.exp(heights), shape[axis_at] // blocks).reshape((-1,) + (1,) * (len(shape) - 1 - axis_at))
    return factor_of


def shared_out(own_key, own, number, rows, count, top, most, skew):
    ranking = jax.random.permutation(own_key, count)
    packed, ordinary = shares(count, rows * top, most, skew, True), shares(count, rows * top, most, skew, False)
    places = jnp.arange(count)

    def named(sizes, rotation):
        used = int((sizes > 0).sum())
        fixed = max(1, used // 4)
        moved = fixed + (places - fixed + rotation * (used - fixed)) % max(1, count - fixed)
        return jnp.zeros((count,), jnp.int32).at[ranking[jnp.where(places < fixed, places, moved)]].set(jnp.asarray(sizes, jnp.int32))

    sizes = jnp.where(number % 4 == 0, named(packed, number // 4), named(ordinary, number - number // 4 - 1))
    mixed = jax.random.permutation(jax.random.fold_in(own, 3), count)
    source_of, receiver = mixed[0:count // 2 * 2:2], mixed[1:count // 2 * 2:2]
    slack = jnp.minimum(sizes[source_of] - 1, most - sizes[receiver]) // 2
    slack = jnp.where((source_of == ranking[0]) | (receiver == ranking[0]) | (sizes[receiver] == 0), 0, jnp.maximum(slack, 0))
    moved = jax.random.randint(jax.random.fold_in(own, 4), (count // 2,), 0, 1 << 20) % (slack + 1)
    sizes = sizes.at[source_of].add(-moved).at[receiver].add(moved)
    members = jnp.searchsorted(jnp.cumsum(sizes), jnp.arange(rows * top), side="right").astype(jnp.int32)
    grid = members.reshape(top, rows).T
    grid = grid[jax.random.permutation(jax.random.fold_in(own, 1), rows)]
    rotation = jax.random.randint(jax.random.fold_in(own, 2), (rows, 1), 0, top)
    return jnp.take_along_axis(grid, (jnp.arange(top)[None, :] + rotation) % top, axis=1)


def shares(count, total, most, lean, full):
    portions = [(1 << 20) // math.isqrt(rank ** lean) + 1 for rank in range(1, count + 1)]
    largest = most if full else min(most, max(-(-total // count), total * portions[0] // sum(portions)))
    least = 1 if total - largest >= count - 1 else 0
    counts, spare = [largest] + [least] * (count - 1), total - largest - least * (count - 1)
    while spare > 0:
        free = [i for i in range(1, count) if counts[i] < largest] or [i for i in range(1, count) if counts[i] < most]
        pool, remaining = sum([portions[i] for i in free]), spare
        for i in free:
            addition = min(most - counts[i], max(1, remaining * portions[i] // pool), spare)
            counts[i] = counts[i] + addition
            spare = spare - addition
    return np.array(counts)


def normal_values(stream_key, dims, spread, reach, shards=(), kind=jnp.bfloat16):
    result = jax.random.normal(stream_key, dims, jnp.float32) * spread
    if len(shards) > 0:
        result = steps_of(stream_key, dims, shards, -0.22, 0.18) * result
    return jnp.clip(result, min=-reach, max=reach).astype(kind)


def setup_inputs(seed: int = 0, part: int = 0) -> dict:
    streams_of = jax.random.split(jax.random.key(seed), 15)
    own_keys = jax.random.split(jax.random.fold_in(streams_of[14], part), 15)
    queries = draw_queries(jax.random.fold_in(jax.random.fold_in(streams_of[14], part), 71), part)
    cache_keys = draw_cache_keys(jax.random.fold_in(jax.random.fold_in(streams_of[14], part), 71), part)
    cache_values = normal_values(own_keys[2], (REQS * NBLK, BLK, KVH * HD), 1.0, 6.0, ((0, 8), (2, 2)))
    fresh_keys = normal_values(own_keys[3], (REQS, KVH * HD), 1.2, 7.0, ((0, 8), (1, 2)))
    fresh_values = normal_values(own_keys[4], (REQS, KVH * HD), 1.0, 6.0, ((0, 8), (1, 2)))
    block_table = draw_block_table(jax.random.fold_in(jax.random.fold_in(streams_of[14], part), 71), part)
    lengths = draw_lengths(jax.random.fold_in(jax.random.fold_in(streams_of[14], part), 71), part)
    stream = normal_values(own_keys[7], (REQS, D), 0.3, 2.0, ((0, 8),))
    norm_gain = jnp.clip(1.0 + 0.18 * jax.random.normal(streams_of[8], (D,), jnp.float32), 0.099609375, 1.8984375).astype(jnp.bfloat16)
    router = normal_values(streams_of[9], (D, EXPERTS), D ** -0.5, 0.078125)
    routes_keys = jax.random.split(jax.random.fold_in(own_keys[10], 1), REQS // TOK_DEV)
    routes_turns = jax.random.permutation(jax.random.fold_in(own_keys[10], 3), REQS // TOK_DEV)
    routes = jax.vmap(lambda own, number: shared_out(jax.random.fold_in(own_keys[10], 2), own, number, TOK_DEV, EXPERTS, 2, CAP, 2))(routes_keys, routes_turns).reshape((REQS, 2))
    expert_gate = normal_values(streams_of[11], (D, EXPERTS * FFW), D ** -0.5, 0.078125, ((1, 16),))
    expert_up = normal_values(streams_of[12], (D, EXPERTS * FFW), D ** -0.5, 0.078125, ((1, 16),))
    expert_down = normal_values(streams_of[13], (EXPERTS * FFW, D), FFW ** -0.5, 0.0625, ((0, 16),))
    return dict(queries=queries, cache_keys=cache_keys, cache_values=cache_values, fresh_keys=fresh_keys, fresh_values=fresh_values, block_table=block_table, lengths=lengths, stream=stream, norm_gain=norm_gain, router=router, routes=routes, expert_gate=expert_gate, expert_up=expert_up, expert_down=expert_down)


EPSILON = 1e-05

def logical_cache(pool_keys, pool_values, table, lengths, fresh_keys, fresh_values):
    requests, blocks = table.shape
    width = pool_keys.shape[2]
    context = blocks * pool_keys.shape[1]
    flat = table.reshape(-1)
    keys = pool_keys[flat].reshape(requests, context, width)
    values = pool_values[flat].reshape(requests, context, width)
    position = lax.broadcasted_iota(jnp.int32, (requests, context, 1), 1)
    limit = lengths.reshape(requests, 1, 1)
    keys = jnp.where(position < limit, keys, jnp.where(position == limit, fresh_keys[:, None, :], jnp.zeros_like(keys)))
    values = jnp.where(position < limit, values, jnp.where(position == limit, fresh_values[:, None, :], jnp.zeros_like(values)))
    return (keys, values)

def attend(query, keys, values, limit):
    requests, context, width = keys.shape
    groups = width // HD
    heads = query.shape[1] // HD
    share = heads // groups
    q_heads = query.astype(jnp.float32).reshape(requests, groups, share, HD)
    k_heads = keys.astype(jnp.float32).reshape(requests, context, groups, HD)
    v_heads = values.astype(jnp.float32).reshape(requests, context, groups, HD)
    scores = jnp.einsum('rgqd,rpgd->rgqp', q_heads, k_heads) * HD ** (-0.5)
    position = lax.broadcasted_iota(jnp.int32, scores.shape, 3)
    scores = jnp.where(position <= limit.reshape(requests, 1, 1, 1), scores, -1e+30)
    top = lax.optimization_barrier(jnp.max(scores, axis=3, keepdims=True))
    powers = jnp.exp(scores - top)
    probs = (powers / lax.optimization_barrier(jnp.sum(powers, axis=3, keepdims=True))).astype(jnp.bfloat16)
    mixed = jnp.einsum('rgqp,rpgd->rgqd', probs.astype(jnp.float32), v_heads)
    return mixed.astype(jnp.bfloat16).reshape(requests, heads * HD)

def reference(queries, cache_keys, cache_values, fresh_keys, fresh_values, block_table, lengths, stream, norm_gain, router, routes, expert_gate, expert_up, expert_down):
    slot = jnp.arange(REQS, dtype=jnp.int32)
    owner = slot // TOK_DEV
    table = block_table + (owner * (TOK_DEV * NBLK))[:, None]
    keys, values = logical_cache(cache_keys, cache_values, table, lengths, fresh_keys, fresh_values)
    attn = attend(queries, keys, values, lengths)
    partner = (owner + N_RANKS // 2) % N_RANKS
    served = jnp.where(slot % TOK_DEV == 0, partner * TOK_DEV, slot)
    movers = jnp.arange(N_RANKS, dtype=jnp.int32)
    source = (movers + N_RANKS // 2) % N_RANKS * TOK_DEV
    moved_keys = keys[source]
    moved_values = values[source]
    middle = (stream[served].astype(jnp.float32) + attn[served].astype(jnp.float32)).astype(jnp.bfloat16)
    wide = middle.astype(jnp.float32)
    normed = (wide * lax.rsqrt(lax.optimization_barrier(jnp.mean(wide * wide, axis=1, keepdims=True)) + EPSILON) * norm_gain.astype(jnp.float32)).astype(jnp.bfloat16)
    logits = jnp.dot(normed, router, preferred_element_type=jnp.float32)
    first = jnp.take_along_axis(logits, routes[:, 0:1], axis=1)[:, 0]
    second = jnp.take_along_axis(logits, routes[:, 1:2], axis=1)[:, 0]
    share_first = jax.nn.sigmoid(first - second)
    expert_ids = jnp.arange(EXPERTS, dtype=jnp.int32)
    chosen_first = routes[:, 0:1] == expert_ids[None, :]
    chosen_second = routes[:, 1:2] == expert_ids[None, :]
    member = (chosen_first | chosen_second).astype(jnp.int32)
    gating = jnp.where(chosen_first, share_first[:, None], jnp.float32(0.0)) + jnp.where(chosen_second, (1.0 - share_first)[:, None], jnp.float32(0.0))
    place = jnp.cumsum(member.reshape(N_RANKS, TOK_DEV, EXPERTS), axis=1) - 1
    slot_ids = jnp.arange(CAP, dtype=jnp.int32)
    hit = (member.reshape(N_RANKS, TOK_DEV, EXPERTS, 1) == 1) & (place[..., None] == slot_ids)
    rows_for = lax.optimization_barrier(jnp.sum(jnp.where(hit, slot.reshape(N_RANKS, TOK_DEV, 1, 1), 0), axis=1)).astype(jnp.int32)
    gate_for = lax.optimization_barrier(jnp.sum(jnp.where(hit, gating.reshape(N_RANKS, TOK_DEV, EXPERTS, 1), jnp.float32(0.0)), axis=1))

    def one_expert(index):
        rows = normed[rows_for[:, index].reshape(-1)].astype(jnp.float32)
        start = (index * FFW).astype(jnp.int32)
        w_gate = lax.dynamic_slice_in_dim(expert_gate, start, FFW, 1).astype(jnp.float32)
        w_up = lax.dynamic_slice_in_dim(expert_up, start, FFW, 1).astype(jnp.float32)
        w_down = lax.dynamic_slice_in_dim(expert_down, start, FFW, 0).astype(jnp.float32)
        gate_val = jnp.dot(rows, w_gate, preferred_element_type=jnp.float32)
        up_val = jnp.dot(rows, w_up, preferred_element_type=jnp.float32)
        hidden = (jax.nn.silu(gate_val) * up_val).astype(jnp.bfloat16).astype(jnp.float32)
        return jnp.dot(hidden, w_down, preferred_element_type=jnp.float32)
    outputs = lax.map(one_expert, expert_ids).reshape(EXPERTS, N_RANKS, CAP, D)
    weights = jnp.transpose(gate_for, (1, 0, 2))
    targets = jnp.transpose(rows_for, (1, 0, 2)).reshape(-1)
    moe = jnp.zeros((REQS, D), jnp.float32).at[targets].add((weights[..., None] * outputs).reshape(-1, D))
    layer_out = (middle.astype(jnp.float32) + moe).astype(jnp.bfloat16)
    return (layer_out, moved_keys, moved_values)
```

```python
import functools

import jax
import jax.numpy as jnp
from jax import lax
from jax.experimental import pallas as pl
from jax.experimental.pallas import tpu as pltpu
from jax.sharding import PartitionSpec as P

HD = 128
EPSILON = 1e-05
F32 = jnp.float32
BF16 = jnp.bfloat16
MESH = pl.DeviceIdType.MESH
SLOTS = 8


def iota(shape, axis):
    return lax.broadcasted_iota(jnp.int32, shape, axis)


def kernel(
    sizes,
    table, lens, q_ref, pk_ref, pv_ref, fk_ref, fv_ref, stream_ref, gain_ref,
    router_ref, ext_ref, gate_hbm, up_hbm, down_hbm,
    out_ref, mk_ref, mv_ref,
    wbuf, kv0, attn_s, tok_a, tok_b, normed_s, e1_s, e2_s, hid_s,
    sib_s, sib_r, ret_s, ret_r,
    w_sem, d_sem, bar_a_send, bar_a_recv, tok_b_send, tok_b_recv,
    sib_send, sib_recv, ret_send, ret_recv, mv_send, mv_recv,
):
    ranks, experts, requests, ctx, blk, groups, share, depth, hidden, fc, slots = sizes
    half = depth // 2
    quarter = half // 2
    me = lax.axis_index("ranks")
    tp = lax.axis_index("tp")
    other = 1 - tp
    partner = lax.rem(me + ranks // 2, ranks)
    tokens = ranks * requests
    chunks = hidden // fc
    stacked = depth // hidden
    cols = depth // fc
    nj = cols // 2
    nm = nj // 2

    barrier = pltpu.get_barrier_semaphore()

    def greet(d, _):
        pl.semaphore_signal(
            barrier, inc=1, device_id={"ranks": lax.rem(me + d, ranks)}, device_id_type=MESH
        )
        return 0

    lax.fori_loop(1, ranks, greet, 0)
    pl.semaphore_signal(barrier, inc=1, device_id={"tp": other}, device_id_type=MESH)

    def gu_copy(u):
        src = gate_hbm if u % 2 == 0 else up_hbm
        return pltpu.make_async_copy(
            src.at[:, pl.ds((u // 2) * fc, fc)], wbuf.at[u % slots], w_sem.at[u]
        )

    def d_copy(n):
        at = (
            (other * nj + n) if n < nj else (tp * nj + (n - nj))
        )
        u = 2 * chunks + n // stacked
        return pltpu.make_async_copy(
            down_hbm.at[:, pl.ds(pl.multiple_of(at * fc, fc), fc)],
            wbuf.at[u % slots, pl.ds((n % stacked) * hidden, hidden)],
            d_sem.at[n],
        )

    def start_unit(u):
        if u < 2 * chunks:
            gu_copy(u).start()
        else:
            first = (u - 2 * chunks) * stacked
            for n in range(first, min(first + stacked, cols)):
                d_copy(n).start()

    units = 2 * chunks + -(-cols // stacked)
    for u in range(min(slots, units)):
        start_unit(u)
    started = min(slots, units)

    def attend(i, _):
        limit = lens[i]
        pos = iota((ctx, groups * HD), 0)
        row = iota((requests, groups * HD), 0)

        def logical(pool, fresh):
            x = jnp.concatenate(
                [pool[table[i, j]].astype(F32) for j in range(ctx // blk)], axis=0
            )
            new = jnp.sum(jnp.where(row == i, fresh[...].astype(F32), 0.0), axis=0, keepdims=True)
            return jnp.where(pos < limit, x, jnp.where(pos == limit, new, 0.0)).astype(BF16)

        keys = logical(pk_ref, fk_ref)
        values = logical(pv_ref, fv_ref)

        @pl.when(i == 0)
        def _():
            kv0[0] = keys
            kv0[1] = values

        for g in range(groups):
            q = q_ref[i, g]
            s = lax.dot_general(
                q, keys[:, g * HD:(g + 1) * HD], (((1,), (1,)), ((), ())),
                preferred_element_type=F32,
            ) * HD ** (-0.5)
            s = jnp.where(iota(s.shape, 1) <= limit, s, -1e30)
            p = jnp.exp(s - jnp.max(s, axis=1, keepdims=True))
            p = (p / jnp.sum(p, axis=1, keepdims=True)).astype(BF16)
            o = jnp.dot(p, values[:, g * HD:(g + 1) * HD], preferred_element_type=F32)
            for h in range(share):
                attn_s[g * share + h, pl.ds(i, 1), :] = o[h:h + 1, :]
        return 0

    lax.fori_loop(0, requests, attend, 0)

    own = stream_ref[:, pl.ds(pl.multiple_of(tp * half, half), half)].astype(F32)
    attn = jnp.concatenate([attn_s[h] for h in range(groups * share)], axis=1)
    mid = own + attn.astype(BF16).astype(F32)
    tok_a[me, :, :quarter] = jnp.concatenate(
        [mid[:, :quarter], mid[:, quarter:]], axis=0
    ).astype(BF16)
    tok_a[me, :, quarter:] = ext_ref[...]

    pl.semaphore_wait(barrier, ranks)

    def a_copy(p, src):
        return pltpu.make_async_remote_copy(
            src_ref=tok_a.at[src], dst_ref=tok_a.at[src],
            send_sem=bar_a_send.at[p], recv_sem=bar_a_recv.at[src],
            device_id={"ranks": p}, device_id_type=MESH,
        )

    def b_copy(r):
        return pltpu.make_async_remote_copy(
            src_ref=tok_a.at[r], dst_ref=tok_b.at[r],
            send_sem=tok_b_send.at[r], recv_sem=tok_b_recv.at[r],
            device_id={"tp": other}, device_id_type=MESH,
        )

    def send_a(d, _):
        a_copy(lax.rem(me + d, ranks), me).start()
        return 0

    lax.fori_loop(1, ranks, send_a, 0)
    b_copy(me).start()

    def forward(d, _):
        r = lax.rem(me + ranks - d, ranks)
        a_copy(r, r).wait_recv()
        b_copy(r).start()
        return 0

    lax.fori_loop(1, ranks, forward, 0)

    moved = [
        pltpu.make_async_remote_copy(
            src_ref=kv0.at[n], dst_ref=ref.at[0],
            send_sem=mv_send.at[n], recv_sem=mv_recv.at[n],
            device_id={"ranks": partner}, device_id_type=MESH,
        )
        for n, ref in enumerate((mk_ref, mv_ref))
    ]

    def wait_b(r, _):
        b_copy(r).wait_recv()
        return 0

    lax.fori_loop(0, ranks, wait_b, 0)
    for copy in moved:
        copy.start()

    def served(tok, r):
        swap = lax.rem(iota((2 * requests, quarter), 0), requests) == 0
        far = tok[lax.rem(r + ranks // 2, ranks), :, :quarter].astype(F32)
        x = jnp.where(swap, far, tok[r, :, :quarter].astype(F32))
        return x[:requests], x[requests:]

    at_a = pl.multiple_of(tp * half, half)
    at_b = pl.multiple_of(other * half, half)
    places = (
        at_a, pl.multiple_of(at_a + quarter, quarter),
        at_b, pl.multiple_of(at_b + quarter, quarter),
    )

    def normalise(m, _):
        rows = []
        for r in (2 * m, 2 * m + 1):
            parts = served(tok_a, r) + served(tok_b, r)
            square = sum(jnp.sum(x * x, axis=1, keepdims=True) for x in parts)
            scale = lax.rsqrt(square / depth + EPSILON)
            rows.append([x * scale for x in parts])
            ext = tok_a[r, :, quarter:].astype(F32)
            base = pl.multiple_of(r * requests, requests)
            e1_s[pl.ds(base, requests), :] = ext[:requests]
            e2_s[pl.ds(base, requests), :] = ext[requests:]
        span = pl.ds(pl.multiple_of(m * 2 * requests, 2 * requests), 2 * requests)
        for n, place in enumerate(places):
            x = jnp.concatenate([rows[0][n], rows[1][n]], axis=0)
            gain = gain_ref[:, pl.ds(place, quarter)].astype(F32)
            normed_s[span, pl.ds(place, quarter)] = (x * gain).astype(BF16)
        return 0

    lax.fori_loop(0, ranks // 2, normalise, 0)

    logits = lax.dot_general(
        normed_s[...], router_ref[...], (((1,), (1,)), ((), ())), preferred_element_type=F32
    )
    lane = iota(logits.shape, 1).astype(F32)
    e1, e2 = e1_s[:, :1], e2_s[:, :1]
    first = jnp.sum(jnp.where(lane == e1, logits, 0.0), axis=1, keepdims=True)
    second = jnp.sum(jnp.where(lane == e2, logits, 0.0), axis=1, keepdims=True)
    share1 = jax.nn.sigmoid(first - second)
    mine = (me // (ranks // experts)).astype(F32)
    weight = jnp.where(e1 == mine, share1, 0.0) + jnp.where(e2 == mine, 1.0 - share1, 0.0)

    kstep = depth // 3
    for c in range(chunks):
        gu_copy(2 * c).wait()
        gu_copy(2 * c + 1).wait()
        gs, us = (2 * c) % slots, (2 * c + 1) % slots

        def step(k, acc):
            span = pl.ds(pl.multiple_of(k * kstep, kstep), kstep)
            x = normed_s[:, span]
            return (
                acc[0] + jnp.dot(x, wbuf[gs, span, :], preferred_element_type=F32),
                acc[1] + jnp.dot(x, wbuf[us, span, :], preferred_element_type=F32),
            )

        zero = jnp.zeros((tokens, fc), F32)
        g, u = lax.fori_loop(0, 3, step, (zero, zero))
        hid_s[:, c * fc:(c + 1) * fc] = (jax.nn.silu(g) * u).astype(BF16)
        for _ in range(2):
            if started < units:
                start_unit(started)
                started += 1
    assert started == units

    def sib_copy(j):
        return pltpu.make_async_remote_copy(
            src_ref=sib_s.at[j], dst_ref=sib_r.at[j],
            send_sem=sib_send.at[j], recv_sem=sib_recv.at[j],
            device_id={"tp": other}, device_id_type=MESH,
        )

    def ret_copy(m, p, src):
        return pltpu.make_async_remote_copy(
            src_ref=ret_s.at[m, p], dst_ref=ret_r.at[m, src],
            send_sem=ret_send.at[m, p], recv_sem=ret_recv.at[m, src],
            device_id={"ranks": p}, device_id_type=MESH,
        )

    held = None
    for n in range(cols):
        d_copy(n).wait()
        slot = (2 * chunks + n // stacked) % slots
        w = wbuf[slot, (n % stacked) * hidden:(n % stacked + 1) * hidden, :]
        y = jnp.dot(hid_s[...], w, preferred_element_type=F32) * weight
        if n < nj:
            sib_s[n] = y.astype(BF16)
            sib_copy(n).start()
            continue
        j = n - nj
        sib_copy(j).wait_recv()
        y = (y + sib_r[j].astype(F32)).reshape(ranks, requests, fc)
        if j % 2 == 0:
            held = y
            continue
        m = j // 2
        ret_s[m] = jnp.concatenate([held, y], axis=1).astype(BF16)

        def send_ret(d, _, m=m):
            p = lax.rem(me + d, ranks)
            ret_copy(m, p, me).start()
            return 0

        lax.fori_loop(1, ranks, send_ret, 0)

    lo, hi = served(tok_a, me)
    mid_now = jnp.concatenate([lo, hi], axis=1)
    for m in range(nm):
        def gather(d, total, m=m):
            r = lax.rem(me + ranks - d, ranks)
            ret_copy(m, r, r).wait_recv()
            return total + ret_r[m, r].astype(F32)

        total = lax.fori_loop(1, ranks, gather, ret_s[m, me].astype(F32))
        for b in range(2):
            span = slice((2 * m + b) * fc, (2 * m + b + 1) * fc)
            out_ref[:, span] = (
                mid_now[:, span] + total[b * requests:(b + 1) * requests]
            ).astype(BF16)

    def drain(d, _):
        p = lax.rem(me + d, ranks)
        a_copy(p, me).wait_send()
        for m in range(nm):
            ret_copy(m, p, me).wait_send()
        return 0

    lax.fori_loop(1, ranks, drain, 0)

    def drain_b(r, _):
        b_copy(r).wait_send()
        return 0

    lax.fori_loop(0, ranks, drain_b, 0)
    for j in range(nj):
        sib_copy(j).wait_send()
    for copy in moved:
        copy.wait()


def shards(
    ranks, queries, cache_keys, cache_values, fresh_keys, fresh_values, block_table, lengths,
    stream, norm_gain, router, routes, expert_gate, expert_up, expert_down,
):
    requests, half = queries.shape
    depth = 2 * half
    experts = router.shape[1]
    blk, width = cache_keys.shape[1:]
    ctx = block_table.shape[1] * blk
    groups = width // HD
    share = half // HD // groups
    hidden = expert_gate.shape[1]
    fc = min(512, hidden)
    chunks = hidden // fc
    cols = depth // fc
    nj = cols // 2
    nm = nj // 2
    quarter = half // 2
    tokens = ranks * requests
    units = 2 * chunks + -(-cols // (depth // hidden))
    slots = min(SLOTS, units)
    q = jnp.pad(
        queries.reshape(requests, groups, share, HD), ((0, 0), (0, 0), (0, 16 - share), (0, 0))
    )
    router_t = jnp.pad(router.T, ((0, 16 - experts), (0, 0)))
    ext = jnp.broadcast_to(routes.T.reshape(2 * requests, 1), (2 * requests, 128)).astype(BF16)
    sizes = (ranks, experts, requests, ctx, blk, groups, share, depth, hidden, fc, slots)
    vmem = pl.BlockSpec(memory_space=pltpu.VMEM)
    smem = pl.BlockSpec(memory_space=pltpu.SMEM)
    hbm = pl.BlockSpec(memory_space=pl.ANY)
    dma = pltpu.SemaphoreType.DMA
    tok = quarter + 128
    moved = jax.ShapeDtypeStruct((1, ctx, width), BF16)
    return pl.pallas_call(
        functools.partial(kernel, sizes),
        out_shape=(jax.ShapeDtypeStruct((requests, half), BF16), moved, moved),
        in_specs=[smem, smem] + [vmem] * 9 + [hbm] * 3,
        out_specs=(vmem, hbm, hbm),
        scratch_shapes=[
            pltpu.VMEM((slots, depth, fc), BF16),
            pltpu.VMEM((2, ctx, width), BF16),
            pltpu.VMEM((half // HD, requests, HD), F32),
            pltpu.VMEM((ranks, 2 * requests, tok), BF16),
            pltpu.VMEM((ranks, 2 * requests, tok), BF16),
            pltpu.VMEM((tokens, depth), BF16),
            pltpu.VMEM((tokens, 128), F32),
            pltpu.VMEM((tokens, 128), F32),
            pltpu.VMEM((tokens, hidden), BF16),
            pltpu.VMEM((nj, tokens, fc), BF16),
            pltpu.VMEM((nj, tokens, fc), BF16),
            pltpu.VMEM((nm, ranks, 2 * requests, fc), BF16),
            pltpu.VMEM((nm, ranks, 2 * requests, fc), BF16),
            dma((2 * chunks,)),
            dma((cols,)),
            dma((ranks,)),
            dma((ranks,)),
            dma((ranks,)),
            dma((ranks,)),
            dma((nj,)),
            dma((nj,)),
            dma((nm, ranks)),
            dma((nm, ranks)),
            dma((2,)),
            dma((2,)),
        ],
        compiler_params=pltpu.CompilerParams(
            collective_id=0, has_side_effects=True, vmem_limit_bytes=62 * 1024 * 1024
        ),
    )(
        block_table, lengths, q, cache_keys, cache_values, fresh_keys, fresh_values, stream,
        norm_gain.reshape(1, depth), router_t, ext, expert_gate, expert_up, expert_down,
    )


def solution(mesh):
    rows = ("groups", "ranks")
    return jax.shard_map(
        functools.partial(shards, mesh.shape["ranks"]),
        mesh=mesh,
        in_specs=(
            P(rows, "tp"), P(rows, None, "tp"), P(rows, None, "tp"), P(rows, "tp"),
            P(rows, "tp"), P(rows, None), P(rows), P(rows, None), P(), P(), P(rows, None),
            P(None, ("ranks", "tp")), P(None, ("ranks", "tp")), P(("ranks", "tp"), None),
        ),
        out_specs=(P(rows, "tp"), P(rows, None, "tp"), P(rows, None, "tp")),
        check_vma=False,
    )
```

```python
import functools

import jax
import jax.numpy as jnp
from jax import lax
from jax.experimental import pallas as pl
from jax.experimental.pallas import tpu as pltpu
from jax.sharding import PartitionSpec as P

HD = 128
EPSILON = 1e-05
F32 = jnp.float32
BF16 = jnp.bfloat16
MESH = pl.DeviceIdType.MESH
SLOTS = 9


def iota(shape, axis):
    return lax.broadcasted_iota(jnp.int32, shape, axis)


def kernel(
    sizes,
    table, lens, q_ref, pk_ref, pv_ref, fk_ref, fv_ref, stream_ref, gain_ref,
    router_ref, routes, gate_hbm, up_hbm, down_hbm,
    out_ref, mk_ref, mv_ref,
    wbuf, kv0, q_s, gain_s, router_s, attn_s, tok_a, tok_b, normed_s, e1_s, e2_s, hid_s,
    sib_s, sib_r, ret_s, ret_r,
    w_sem, d_sem, bar_a_send, bar_a_recv, tok_b_send, tok_b_recv,
    sib_send, sib_recv, ret_send, ret_recv, mv_send, mv_recv,
):
    ranks, experts, requests, ctx, blk, groups, share, depth, hidden, fc, slots = sizes
    half = depth // 2
    quarter = half // 2
    me = lax.axis_index("ranks")
    tp = lax.axis_index("tp")
    other = 1 - tp
    partner = lax.rem(me + ranks // 2, ranks)
    tokens = ranks * requests
    chunks = hidden // fc
    stacked = depth // hidden
    cols = depth // fc
    nj = cols // 2
    nm = nj // 2

    barrier = pltpu.get_barrier_semaphore()

    def greet(d, _):
        pl.semaphore_signal(
            barrier, inc=1, device_id={"ranks": lax.rem(me + d, ranks)}, device_id_type=MESH
        )
        return 0

    lax.fori_loop(1, ranks, greet, 0)
    pl.semaphore_signal(barrier, inc=1, device_id={"tp": other}, device_id_type=MESH)

    def gu_copy(u):
        src = gate_hbm if u % 2 == 0 else up_hbm
        return pltpu.make_async_copy(
            src.at[:, pl.ds((u // 2) * fc, fc)], wbuf.at[u % slots], w_sem.at[u]
        )

    def d_copy(n):
        at = (
            (other * nj + n) if n < nj else (tp * nj + (n - nj))
        )
        u = 2 * chunks + n // stacked
        return pltpu.make_async_copy(
            down_hbm.at[:, pl.ds(pl.multiple_of(at * fc, fc), fc)],
            wbuf.at[u % slots, pl.ds((n % stacked) * hidden, hidden)],
            d_sem.at[n],
        )

    def start_unit(u):
        if u < 2 * chunks:
            gu_copy(u).start()
        else:
            first = (u - 2 * chunks) * stacked
            for n in range(first, min(first + stacked, cols)):
                d_copy(n).start()

    units = 2 * chunks + -(-cols // stacked)
    for u in range(min(slots, units)):
        start_unit(u)
    started = min(slots, units)

    q_s[...] = jnp.zeros_like(q_s)
    for h in range(groups * share):
        q_s[h // share, :, h % share, :] = q_ref[:, h * HD:(h + 1) * HD].astype(F32)
    gains = gain_ref[...].astype(F32)
    for k in range(depth // 128):
        gain_s[:, k * 128:(k + 1) * 128] = gains[k:k + 1]
    router_s[...] = jnp.zeros_like(router_s)
    router_s[:experts] = router_ref[...].astype(F32)

    def attend(i, _):
        limit = lens[i]
        pos = iota((ctx, groups * HD), 0)
        row = iota((requests, groups * HD), 0)

        def logical(pool, fresh):
            x = jnp.concatenate(
                [pool[table[i, j]].astype(F32) for j in range(ctx // blk)], axis=0
            )
            new = jnp.sum(jnp.where(row == i, fresh[...].astype(F32), 0.0), axis=0, keepdims=True)
            return jnp.where(pos < limit, x, jnp.where(pos == limit, new, 0.0)).astype(BF16)

        keys = logical(pk_ref, fk_ref)
        values = logical(pv_ref, fv_ref)

        @pl.when(i == 0)
        def _():
            kv0[0] = keys
            kv0[1] = values

        for g in range(groups):
            q = q_s[g, i].astype(BF16)
            s = lax.dot_general(
                q, keys[:, g * HD:(g + 1) * HD], (((1,), (1,)), ((), ())),
                preferred_element_type=F32,
            ) * HD ** (-0.5)
            s = jnp.where(iota(s.shape, 1) <= limit, s, -1e30)
            p = jnp.exp(s - jnp.max(s, axis=1, keepdims=True))
            p = (p / jnp.sum(p, axis=1, keepdims=True)).astype(BF16)
            o = jnp.dot(p, values[:, g * HD:(g + 1) * HD], preferred_element_type=F32)
            for h in range(share):
                attn_s[g * share + h, pl.ds(i, 1), :] = o[h:h + 1, :]
        return 0

    lax.fori_loop(0, requests, attend, 0, unroll=4)

    own = stream_ref[:, pl.ds(pl.multiple_of(tp * half, half), half)].astype(F32)
    attn = jnp.concatenate([attn_s[h] for h in range(groups * share)], axis=1)
    mid = own + attn.astype(BF16).astype(F32)
    tok_a[me, :, :quarter] = jnp.concatenate(
        [mid[:, :quarter], mid[:, quarter:]], axis=0
    ).astype(BF16)
    which = iota((2 * requests, 128), 0)
    ext = jnp.zeros((2 * requests, 128), F32)
    for t in range(requests):
        for e in range(2):
            ext = jnp.where(which == e * requests + t, routes[e, t].astype(F32), ext)
    tok_a[me, :, quarter:] = ext.astype(BF16)

    pl.semaphore_wait(barrier, ranks)

    def mate_of(r):
        return r + 1 - 2 * lax.rem(r, 2)

    mate = mate_of(me)

    def a_copy(p, src, s):
        return pltpu.make_async_remote_copy(
            src_ref=tok_a.at[src], dst_ref=tok_a.at[src],
            send_sem=bar_a_send.at[s], recv_sem=bar_a_recv.at[src],
            device_id={"ranks": p}, device_id_type=MESH,
        )

    def b_copy(r):
        return pltpu.make_async_remote_copy(
            src_ref=tok_a.at[r], dst_ref=tok_b.at[r],
            send_sem=tok_b_send.at[r], recv_sem=tok_b_recv.at[r],
            device_id={"tp": other}, device_id_type=MESH,
        )

    def send_a(d, _):
        p = lax.rem(me + 2 * d, ranks)
        a_copy(p, me, p).start()
        return 0

    lax.fori_loop(1, ranks // 2, send_a, 0)
    a_copy(mate, me, mate).start()
    b_copy(me).start()
    a_copy(mate, mate, mate).wait_recv()
    b_copy(mate).start()

    def forward(d, _):
        r = lax.rem(me + ranks - 2 * d, ranks)
        a_copy(r, r, r).wait_recv()
        a_copy(mate, r, mate_of(r)).start()
        b_copy(r).start()
        return 0

    lax.fori_loop(1, ranks // 2, forward, 0)

    def forward_mate(d, _):
        r = mate_of(lax.rem(me + ranks - 2 * d, ranks))
        a_copy(r, r, r).wait_recv()
        b_copy(r).start()
        return 0

    lax.fori_loop(1, ranks // 2, forward_mate, 0)

    moved = [
        pltpu.make_async_remote_copy(
            src_ref=kv0.at[n], dst_ref=ref.at[0],
            send_sem=mv_send.at[n], recv_sem=mv_recv.at[n],
            device_id={"ranks": partner}, device_id_type=MESH,
        )
        for n, ref in enumerate((mk_ref, mv_ref))
    ]

    def wait_b(r, _):
        b_copy(r).wait_recv()
        return 0

    lax.fori_loop(0, ranks, wait_b, 0)
    for copy in moved:
        copy.start()

    def served(tok, r):
        swap = lax.rem(iota((2 * requests, quarter), 0), requests) == 0
        far = tok[lax.rem(r + ranks // 2, ranks), :, :quarter].astype(F32)
        x = jnp.where(swap, far, tok[r, :, :quarter].astype(F32))
        return x[:requests], x[requests:]

    at_a = pl.multiple_of(tp * half, half)
    at_b = pl.multiple_of(other * half, half)
    places = (
        at_a, pl.multiple_of(at_a + quarter, quarter),
        at_b, pl.multiple_of(at_b + quarter, quarter),
    )

    def normalise(m, _):
        rows = []
        for r in (2 * m, 2 * m + 1):
            parts = served(tok_a, r) + served(tok_b, r)
            square = sum(jnp.sum(x * x, axis=1, keepdims=True) for x in parts)
            scale = lax.rsqrt(square / depth + EPSILON)
            rows.append([x * scale for x in parts])
            ext = tok_a[r, :, quarter:].astype(F32)
            base = pl.multiple_of(r * requests, requests)
            e1_s[pl.ds(base, requests), :] = ext[:requests]
            e2_s[pl.ds(base, requests), :] = ext[requests:]
        span = pl.ds(pl.multiple_of(m * 2 * requests, 2 * requests), 2 * requests)
        for n, place in enumerate(places):
            x = jnp.concatenate([rows[0][n], rows[1][n]], axis=0)
            gain = gain_s[:, pl.ds(place, quarter)]
            normed_s[span, pl.ds(place, quarter)] = (x * gain).astype(BF16)
        return 0

    lax.fori_loop(0, ranks // 2, normalise, 0)

    logits = lax.dot_general(
        normed_s[...], router_s[...].astype(BF16), (((1,), (1,)), ((), ())), preferred_element_type=F32
    )
    lane = iota(logits.shape, 1).astype(F32)
    e1, e2 = e1_s[:, :1], e2_s[:, :1]
    first = jnp.sum(jnp.where(lane == e1, logits, 0.0), axis=1, keepdims=True)
    second = jnp.sum(jnp.where(lane == e2, logits, 0.0), axis=1, keepdims=True)
    share1 = jax.nn.sigmoid(first - second)
    mine = (me // (ranks // experts)).astype(F32)
    weight = jnp.where(e1 == mine, share1, 0.0) + jnp.where(e2 == mine, 1.0 - share1, 0.0)

    kstep = depth // 3
    for c in range(chunks):
        gu_copy(2 * c).wait()
        gu_copy(2 * c + 1).wait()
        gs, us = (2 * c) % slots, (2 * c + 1) % slots

        def step(k, acc):
            span = pl.ds(pl.multiple_of(k * kstep, kstep), kstep)
            x = normed_s[:, span]
            return (
                acc[0] + jnp.dot(x, wbuf[gs, span, :], preferred_element_type=F32),
                acc[1] + jnp.dot(x, wbuf[us, span, :], preferred_element_type=F32),
            )

        zero = jnp.zeros((tokens, fc), F32)
        g, u = lax.fori_loop(0, 3, step, (zero, zero))
        hid_s[:, c * fc:(c + 1) * fc] = (jax.nn.silu(g) * u).astype(BF16)
        for _ in range(2):
            if started < units:
                start_unit(started)
                started += 1
    assert started == units

    def sib_copy(j):
        return pltpu.make_async_remote_copy(
            src_ref=sib_s.at[j], dst_ref=sib_r.at[j],
            send_sem=sib_send.at[j], recv_sem=sib_recv.at[j],
            device_id={"tp": other}, device_id_type=MESH,
        )

    def ret_copy(m, p, src):
        return pltpu.make_async_remote_copy(
            src_ref=ret_s.at[m, p], dst_ref=ret_r.at[m, src],
            send_sem=ret_send.at[m, p], recv_sem=ret_recv.at[m, src],
            device_id={"ranks": p}, device_id_type=MESH,
        )

    held = None
    for n in range(cols):
        d_copy(n).wait()
        slot = (2 * chunks + n // stacked) % slots
        w = wbuf[slot, (n % stacked) * hidden:(n % stacked + 1) * hidden, :]
        y = jnp.dot(hid_s[...], w, preferred_element_type=F32) * weight
        if n < nj:
            sib_s[n] = y.astype(BF16)
            sib_copy(n).start()
            continue
        j = n - nj
        sib_copy(j).wait_recv()
        y = (y + sib_r[j].astype(F32)).reshape(ranks, requests, fc)
        if j % 2 == 0:
            held = y
            continue
        m = j // 2
        ret_s[m] = jnp.concatenate([held, y], axis=1).astype(BF16)

        def send_ret(d, _, m=m):
            p = lax.rem(me + d, ranks)
            ret_copy(m, p, me).start()
            return 0

        lax.fori_loop(1, ranks, send_ret, 0)

    lo, hi = served(tok_a, me)
    mid_now = jnp.concatenate([lo, hi], axis=1)
    for m in range(nm):
        def gather(d, total, m=m):
            r = lax.rem(me + ranks - d, ranks)
            ret_copy(m, r, r).wait_recv()
            return total + ret_r[m, r].astype(F32)

        total = lax.fori_loop(1, ranks, gather, ret_s[m, me].astype(F32))
        for b in range(2):
            span = slice((2 * m + b) * fc, (2 * m + b + 1) * fc)
            out_ref[:, span] = (
                mid_now[:, span] + total[b * requests:(b + 1) * requests]
            ).astype(BF16)

    def drain(d, _):
        p = lax.rem(me + d, ranks)
        for m in range(nm):
            ret_copy(m, p, me).wait_send()
        return 0

    lax.fori_loop(1, ranks, drain, 0)

    def drain_a(d, _):
        p = lax.rem(me + 2 * d, ranks)
        a_copy(p, me, p).wait_send()
        a_copy(mate, p, mate_of(p)).wait_send()
        return 0

    lax.fori_loop(1, ranks // 2, drain_a, 0)
    a_copy(mate, me, mate).wait_send()

    def drain_b(r, _):
        b_copy(r).wait_send()
        return 0

    lax.fori_loop(0, ranks, drain_b, 0)
    for j in range(nj):
        sib_copy(j).wait_send()
    for copy in moved:
        copy.wait()


def deliver(*refs):
    copies = [pltpu.make_async_copy(refs[n], refs[3 + n], refs[6].at[n]) for n in range(3)]
    for copy in copies:
        copy.start()
    for copy in copies:
        copy.wait()


def shards(
    ranks, queries, cache_keys, cache_values, fresh_keys, fresh_values, block_table, lengths,
    stream, norm_gain, router, routes, expert_gate, expert_up, expert_down,
):
    requests, half = queries.shape
    depth = 2 * half
    experts = router.shape[1]
    blk, width = cache_keys.shape[1:]
    ctx = block_table.shape[1] * blk
    groups = width // HD
    share = half // HD // groups
    hidden = expert_gate.shape[1]
    fc = min(512, hidden)
    chunks = hidden // fc
    cols = depth // fc
    nj = cols // 2
    nm = nj // 2
    quarter = half // 2
    tokens = ranks * requests
    units = 2 * chunks + -(-cols // (depth // hidden))
    slots = min(SLOTS, units)
    sizes = (ranks, experts, requests, ctx, blk, groups, share, depth, hidden, fc, slots)
    vmem = pl.BlockSpec(memory_space=pltpu.VMEM)
    smem = pl.BlockSpec(memory_space=pltpu.SMEM)
    hbm = pl.BlockSpec(memory_space=pl.ANY)
    dma = pltpu.SemaphoreType.DMA
    tok = quarter + 128
    moved = jax.ShapeDtypeStruct((1, ctx, width), BF16)
    results = pl.pallas_call(
        functools.partial(kernel, sizes),
        out_shape=(jax.ShapeDtypeStruct((requests, half), BF16), moved, moved),
        in_specs=[smem, smem] + [vmem] * 8 + [smem] + [hbm] * 3,
        out_specs=(vmem, hbm, hbm),
        scratch_shapes=[
            pltpu.VMEM((slots, depth, fc), BF16),
            pltpu.VMEM((2, ctx, width), BF16),
            pltpu.VMEM((groups, requests, 8 * -(-share // 8), HD), F32),
            pltpu.VMEM((1, depth), F32),
            pltpu.VMEM((8 * -(-experts // 8), depth), F32),
            pltpu.VMEM((half // HD, requests, HD), F32),
            pltpu.VMEM((ranks, 2 * requests, tok), BF16),
            pltpu.VMEM((ranks, 2 * requests, tok), BF16),
            pltpu.VMEM((tokens, depth), BF16),
            pltpu.VMEM((tokens, 128), F32),
            pltpu.VMEM((tokens, 128), F32),
            pltpu.VMEM((tokens, hidden), BF16),
            pltpu.VMEM((nj, tokens, fc), BF16),
            pltpu.VMEM((nj, tokens, fc), BF16),
            pltpu.VMEM((nm, ranks, 2 * requests, fc), BF16),
            pltpu.VMEM((nm, ranks, 2 * requests, fc), BF16),
            dma((2 * chunks,)),
            dma((cols,)),
            dma((ranks,)),
            dma((ranks,)),
            dma((ranks,)),
            dma((ranks,)),
            dma((nj,)),
            dma((nj,)),
            dma((nm, ranks)),
            dma((nm, ranks)),
            dma((2,)),
            dma((2,)),
        ],
        compiler_params=pltpu.CompilerParams(
            collective_id=0, has_side_effects=True, vmem_limit_bytes=62 * 1024 * 1024
        ),
    )(
        block_table, lengths, queries, cache_keys, cache_values, fresh_keys, fresh_values, stream,
        norm_gain.reshape(depth // 128, 128), router.T, routes.T,
        expert_gate, expert_up, expert_down,
    )
    return pl.pallas_call(
        deliver,
        out_shape=[jax.ShapeDtypeStruct(x.shape, x.dtype) for x in results],
        in_specs=[hbm] * 3,
        out_specs=[hbm] * 3,
        scratch_shapes=[dma((3,))],
    )(*results)


def solution(mesh):
    rows = ("groups", "ranks")
    return jax.shard_map(
        functools.partial(shards, mesh.shape["ranks"]),
        mesh=mesh,
        in_specs=(
            P(rows, "tp"), P(rows, None, "tp"), P(rows, None, "tp"), P(rows, "tp"),
            P(rows, "tp"), P(rows, None), P(rows), P(rows, None), P(), P(), P(rows, None),
            P(None, ("ranks", "tp")), P(None, ("ranks", "tp")), P(("ranks", "tp"), None),
        ),
        out_specs=(P(rows, "tp"), P(rows, None, "tp"), P(rows, None, "tp")),
        check_vma=False,
    )
```

```python
import functools

import jax
import jax.numpy as jnp
from jax import lax
from jax.experimental import pallas as pl
from jax.experimental.pallas import tpu as pltpu
from jax.sharding import PartitionSpec as P

HD = 128
EPSILON = 1e-05
F32 = jnp.float32
BF16 = jnp.bfloat16
MESH = pl.DeviceIdType.MESH
SLOTS = 9


def iota(shape, axis):
    return lax.broadcasted_iota(jnp.int32, shape, axis)


def kernel(
    sizes,
    table, lens, q_ref, pk_ref, pv_ref, fk_ref, fv_ref, stream_ref, gain_ref,
    router_ref, routes, gate_hbm, up_hbm, down_hbm,
    out_ref, mk_ref, mv_ref,
    wbuf, kv0, q_s, gain_s, router_s, attn_s, tok_a, tok_b, normed_s, e1_s, e2_s, hid_s,
    sib_s, sib_r, ret_s, ret_r,
    w_sem, d_sem, bar_a_send, bar_a_recv, tok_b_send, tok_b_recv,
    sib_send, sib_recv, ret_send, ret_recv, mv_send, mv_recv,
):
    ranks, experts, requests, ctx, blk, groups, share, depth, hidden, fc, slots = sizes
    half = depth // 2
    quarter = half // 2
    me = lax.axis_index("ranks")
    tp = lax.axis_index("tp")
    other = 1 - tp
    partner = lax.rem(me + ranks // 2, ranks)
    tokens = ranks * requests
    chunks = hidden // fc
    stacked = depth // hidden
    cols = depth // fc
    nj = cols // 2
    nm = nj // 2

    barrier = pltpu.get_barrier_semaphore()

    def greet(d, _):
        pl.semaphore_signal(
            barrier, inc=1, device_id={"ranks": lax.rem(me + d, ranks)}, device_id_type=MESH
        )
        return 0

    lax.fori_loop(1, ranks, greet, 0)
    pl.semaphore_signal(barrier, inc=1, device_id={"tp": other}, device_id_type=MESH)

    def gu_copy(u):
        src = gate_hbm if u % 2 == 0 else up_hbm
        return pltpu.make_async_copy(
            src.at[:, pl.ds((u // 2) * fc, fc)], wbuf.at[u % slots], w_sem.at[u]
        )

    def d_copy(n):
        at = (
            (other * nj + n) if n < nj else (tp * nj + (n - nj))
        )
        u = 2 * chunks + n // stacked
        return pltpu.make_async_copy(
            down_hbm.at[:, pl.ds(pl.multiple_of(at * fc, fc), fc)],
            wbuf.at[u % slots, pl.ds((n % stacked) * hidden, hidden)],
            d_sem.at[n],
        )

    def start_unit(u):
        if u < 2 * chunks:
            gu_copy(u).start()
        else:
            first = (u - 2 * chunks) * stacked
            for n in range(first, min(first + stacked, cols)):
                d_copy(n).start()

    units = 2 * chunks + -(-cols // stacked)
    for u in range(min(slots, units)):
        start_unit(u)
    started = min(slots, units)

    q_s[...] = jnp.zeros_like(q_s)
    for h in range(groups * share):
        q_s[h // share, :, h % share, :] = q_ref[:, h * HD:(h + 1) * HD].astype(F32)
    gains = gain_ref[...].astype(F32)
    for k in range(depth // 128):
        gain_s[:, k * 128:(k + 1) * 128] = gains[k:k + 1]
    router_s[...] = jnp.zeros_like(router_s)
    router_s[:experts] = router_ref[...].astype(F32)

    def attend(i, _):
        limit = lens[i]
        pos = iota((ctx, groups * HD), 0)
        row = iota((requests, groups * HD), 0)

        def logical(pool, fresh):
            x = jnp.concatenate(
                [pool[table[i, j]].astype(F32) for j in range(ctx // blk)], axis=0
            )
            new = jnp.sum(jnp.where(row == i, fresh[...].astype(F32), 0.0), axis=0, keepdims=True)
            return jnp.where(pos < limit, x, jnp.where(pos == limit, new, 0.0)).astype(BF16)

        keys = logical(pk_ref, fk_ref)
        values = logical(pv_ref, fv_ref)

        @pl.when(i == 0)
        def _():
            kv0[0] = keys
            kv0[1] = values

        for g in range(groups):
            q = q_s[g, i].astype(BF16)
            s = lax.dot_general(
                q, keys[:, g * HD:(g + 1) * HD], (((1,), (1,)), ((), ())),
                preferred_element_type=F32,
            ) * HD ** (-0.5)
            s = jnp.where(iota(s.shape, 1) <= limit, s, -1e30)
            p = jnp.exp(s - jnp.max(s, axis=1, keepdims=True))
            p = (p / jnp.sum(p, axis=1, keepdims=True)).astype(BF16)
            o = jnp.dot(p, values[:, g * HD:(g + 1) * HD], preferred_element_type=F32)
            for h in range(share):
                attn_s[g * share + h, pl.ds(i, 1), :] = o[h:h + 1, :]
        return 0

    lax.fori_loop(0, requests, attend, 0, unroll=4)

    own = stream_ref[:, pl.ds(pl.multiple_of(tp * half, half), half)].astype(F32)
    attn = jnp.concatenate([attn_s[h] for h in range(groups * share)], axis=1)
    mid = own + attn.astype(BF16).astype(F32)
    tok_a[me, :, :quarter] = jnp.concatenate(
        [mid[:, :quarter], mid[:, quarter:]], axis=0
    ).astype(BF16)
    which = iota((2 * requests, 128), 0)
    ext = jnp.zeros((2 * requests, 128), F32)
    for t in range(requests):
        for e in range(2):
            ext = jnp.where(which == e * requests + t, routes[e, t].astype(F32), ext)
    tok_a[me, :, quarter:] = ext.astype(BF16)

    pl.semaphore_wait(barrier, ranks)

    def mate_of(r):
        return r + 1 - 2 * lax.rem(r, 2)

    mate = mate_of(me)

    def a_copy(p, src, s):
        return pltpu.make_async_remote_copy(
            src_ref=tok_a.at[src], dst_ref=tok_a.at[src],
            send_sem=bar_a_send.at[s], recv_sem=bar_a_recv.at[src],
            device_id={"ranks": p}, device_id_type=MESH,
        )

    def b_copy(r):
        return pltpu.make_async_remote_copy(
            src_ref=tok_a.at[r], dst_ref=tok_b.at[r],
            send_sem=tok_b_send.at[r], recv_sem=tok_b_recv.at[r],
            device_id={"tp": other}, device_id_type=MESH,
        )

    def send_a(d, _):
        p = lax.rem(me + 2 * d, ranks)
        a_copy(p, me, p).start()
        return 0

    lax.fori_loop(1, ranks // 2, send_a, 0)
    a_copy(mate, me, mate).start()
    b_copy(me).start()
    a_copy(mate, mate, mate).wait_recv()
    b_copy(mate).start()

    def forward(d, _):
        r = lax.rem(me + ranks - 2 * d, ranks)
        a_copy(r, r, r).wait_recv()
        a_copy(mate, r, mate_of(r)).start()
        b_copy(r).start()
        return 0

    lax.fori_loop(1, ranks // 2, forward, 0)

    def forward_mate(d, _):
        r = mate_of(lax.rem(me + ranks - 2 * d, ranks))
        a_copy(r, r, r).wait_recv()
        b_copy(r).start()
        return 0

    lax.fori_loop(1, ranks // 2, forward_mate, 0)

    moved = [
        pltpu.make_async_remote_copy(
            src_ref=kv0.at[n], dst_ref=ref.at[0],
            send_sem=mv_send.at[n], recv_sem=mv_recv.at[n],
            device_id={"ranks": partner}, device_id_type=MESH,
        )
        for n, ref in enumerate((mk_ref, mv_ref))
    ]

    def wait_b(r, _):
        b_copy(r).wait_recv()
        return 0

    lax.fori_loop(0, ranks, wait_b, 0)
    for copy in moved:
        copy.start()

    def served(tok, r):
        swap = lax.rem(iota((2 * requests, quarter), 0), requests) == 0
        far = tok[lax.rem(r + ranks // 2, ranks), :, :quarter].astype(F32)
        x = jnp.where(swap, far, tok[r, :, :quarter].astype(F32))
        return x[:requests], x[requests:]

    at_a = pl.multiple_of(tp * half, half)
    at_b = pl.multiple_of(other * half, half)
    places = (
        at_a, pl.multiple_of(at_a + quarter, quarter),
        at_b, pl.multiple_of(at_b + quarter, quarter),
    )

    def normalise(m, _):
        rows = []
        for r in (2 * m, 2 * m + 1):
            parts = served(tok_a, r) + served(tok_b, r)
            square = sum(jnp.sum(x * x, axis=1, keepdims=True) for x in parts)
            scale = lax.rsqrt(square / depth + EPSILON)
            rows.append([x * scale for x in parts])
            ext = tok_a[r, :, quarter:].astype(F32)
            base = pl.multiple_of(r * requests, requests)
            e1_s[pl.ds(base, requests), :] = ext[:requests]
            e2_s[pl.ds(base, requests), :] = ext[requests:]
        span = pl.ds(pl.multiple_of(m * 2 * requests, 2 * requests), 2 * requests)
        for n, place in enumerate(places):
            x = jnp.concatenate([rows[0][n], rows[1][n]], axis=0)
            gain = gain_s[:, pl.ds(place, quarter)]
            normed_s[span, pl.ds(place, quarter)] = (x * gain).astype(BF16)
        return 0

    lax.fori_loop(0, ranks // 2, normalise, 0)

    logits = lax.dot_general(
        normed_s[...], router_s[...].astype(BF16), (((1,), (1,)), ((), ())), preferred_element_type=F32
    )
    lane = iota(logits.shape, 1).astype(F32)
    e1, e2 = e1_s[:, :1], e2_s[:, :1]
    first = jnp.sum(jnp.where(lane == e1, logits, 0.0), axis=1, keepdims=True)
    second = jnp.sum(jnp.where(lane == e2, logits, 0.0), axis=1, keepdims=True)
    share1 = jax.nn.sigmoid(first - second)
    mine = (me // (ranks // experts)).astype(F32)
    weight = jnp.where(e1 == mine, share1, 0.0) + jnp.where(e2 == mine, 1.0 - share1, 0.0)

    kstep = depth // 3
    for c in range(chunks):
        gu_copy(2 * c).wait()
        gu_copy(2 * c + 1).wait()
        gs, us = (2 * c) % slots, (2 * c + 1) % slots

        def step(k, acc):
            span = pl.ds(pl.multiple_of(k * kstep, kstep), kstep)
            x = normed_s[:, span]
            return (
                acc[0] + jnp.dot(x, wbuf[gs, span, :], preferred_element_type=F32),
                acc[1] + jnp.dot(x, wbuf[us, span, :], preferred_element_type=F32),
            )

        zero = jnp.zeros((tokens, fc), F32)
        g, u = lax.fori_loop(0, 3, step, (zero, zero))
        hid_s[:, c * fc:(c + 1) * fc] = (jax.nn.silu(g) * u).astype(BF16)
        for _ in range(2):
            if started < units:
                start_unit(started)
                started += 1
    assert started == units

    def sib_copy(j):
        return pltpu.make_async_remote_copy(
            src_ref=sib_s.at[j], dst_ref=sib_r.at[j],
            send_sem=sib_send.at[j], recv_sem=sib_recv.at[j],
            device_id={"tp": other}, device_id_type=MESH,
        )

    def ret_copy(m, p, src):
        return pltpu.make_async_remote_copy(
            src_ref=ret_s.at[m, p], dst_ref=ret_r.at[m, src],
            send_sem=ret_send.at[m, p], recv_sem=ret_recv.at[m, src],
            device_id={"ranks": p}, device_id_type=MESH,
        )

    held = None
    for n in range(cols):
        d_copy(n).wait()
        slot = (2 * chunks + n // stacked) % slots
        w = wbuf[slot, (n % stacked) * hidden:(n % stacked + 1) * hidden, :]
        y = jnp.dot(hid_s[...], w, preferred_element_type=F32) * weight
        if n < nj:
            sib_s[n] = y.astype(BF16)
            sib_copy(n).start()
            continue
        j = n - nj
        sib_copy(j).wait_recv()
        y = (y + sib_r[j].astype(F32)).reshape(ranks, requests, fc)
        if j % 2 == 0:
            held = y
            continue
        m = j // 2
        ret_s[m] = jnp.concatenate([held, y], axis=1).astype(BF16)

        def send_ret(d, _, m=m):
            p = lax.rem(me + d, ranks)
            ret_copy(m, p, me).start()
            return 0

        lax.fori_loop(1, ranks, send_ret, 0)

    lo, hi = served(tok_a, me)
    mid_now = jnp.concatenate([lo, hi], axis=1)
    for m in range(nm):
        def gather(d, total, m=m):
            r = lax.rem(me + ranks - d, ranks)
            ret_copy(m, r, r).wait_recv()
            return total + ret_r[m, r].astype(F32)

        total = lax.fori_loop(1, ranks, gather, ret_s[m, me].astype(F32))
        for b in range(2):
            span = slice((2 * m + b) * fc, (2 * m + b + 1) * fc)
            out_ref[:, span] = (
                mid_now[:, span] + total[b * requests:(b + 1) * requests]
            ).astype(BF16)

    def drain(d, _):
        p = lax.rem(me + d, ranks)
        for m in range(nm):
            ret_copy(m, p, me).wait_send()
        return 0

    lax.fori_loop(1, ranks, drain, 0)

    def drain_a(d, _):
        p = lax.rem(me + 2 * d, ranks)
        a_copy(p, me, p).wait_send()
        a_copy(mate, p, mate_of(p)).wait_send()
        return 0

    lax.fori_loop(1, ranks // 2, drain_a, 0)
    a_copy(mate, me, mate).wait_send()

    def drain_b(r, _):
        b_copy(r).wait_send()
        return 0

    lax.fori_loop(0, ranks, drain_b, 0)
    for j in range(nj):
        sib_copy(j).wait_send()
    for copy in moved:
        copy.wait()


def deliver(*refs):
    copies = [pltpu.make_async_copy(refs[n], refs[3 + n], refs[6].at[n]) for n in range(3)]
    for copy in copies:
        copy.start()
    for copy in copies:
        copy.wait()


def shards(
    ranks, queries, cache_keys, cache_values, fresh_keys, fresh_values, block_table, lengths,
    stream, norm_gain, router, routes, expert_gate, expert_up, expert_down,
):
    requests, half = queries.shape
    depth = 2 * half
    experts = router.shape[1]
    blk, width = cache_keys.shape[1:]
    ctx = block_table.shape[1] * blk
    groups = width // HD
    share = half // HD // groups
    hidden = expert_gate.shape[1]
    fc = min(512, hidden)
    chunks = hidden // fc
    cols = depth // fc
    nj = cols // 2
    nm = nj // 2
    quarter = half // 2
    tokens = ranks * requests
    units = 2 * chunks + -(-cols // (depth // hidden))
    slots = min(SLOTS, units)
    sizes = (ranks, experts, requests, ctx, blk, groups, share, depth, hidden, fc, slots)
    vmem = pl.BlockSpec(memory_space=pltpu.VMEM)
    smem = pl.BlockSpec(memory_space=pltpu.SMEM)
    hbm = pl.BlockSpec(memory_space=pl.ANY)
    dma = pltpu.SemaphoreType.DMA
    tok = quarter + 128
    moved = jax.ShapeDtypeStruct((1, ctx, width), BF16)
    results = pl.pallas_call(
        functools.partial(kernel, sizes),
        out_shape=(jax.ShapeDtypeStruct((requests, half), BF16), moved, moved),
        in_specs=[smem, smem] + [vmem] * 8 + [smem] + [hbm] * 3,
        out_specs=(vmem, hbm, hbm),
        scratch_shapes=[
            pltpu.VMEM((slots, depth, fc), BF16),
            pltpu.VMEM((2, ctx, width), BF16),
            pltpu.VMEM((groups, requests, 8 * -(-share // 8), HD), F32),
            pltpu.VMEM((1, depth), F32),
            pltpu.VMEM((8 * -(-experts // 8), depth), F32),
            pltpu.VMEM((half // HD, requests, HD), F32),
            pltpu.VMEM((ranks, 2 * requests, tok), BF16),
            pltpu.VMEM((ranks, 2 * requests, tok), BF16),
            pltpu.VMEM((tokens, depth), BF16),
            pltpu.VMEM((tokens, 128), F32),
            pltpu.VMEM((tokens, 128), F32),
            pltpu.VMEM((tokens, hidden), BF16),
            pltpu.VMEM((nj, tokens, fc), BF16),
            pltpu.VMEM((nj, tokens, fc), BF16),
            pltpu.VMEM((nm, ranks, 2 * requests, fc), BF16),
            pltpu.VMEM((nm, ranks, 2 * requests, fc), BF16),
            dma((2 * chunks,)),
            dma((cols,)),
            dma((ranks,)),
            dma((ranks,)),
            dma((ranks,)),
            dma((ranks,)),
            dma((nj,)),
            dma((nj,)),
            dma((nm, ranks)),
            dma((nm, ranks)),
            dma((2,)),
            dma((2,)),
        ],
        compiler_params=pltpu.CompilerParams(
            collective_id=0, has_side_effects=True, vmem_limit_bytes=62 * 1024 * 1024
        ),
    )(
        block_table, lengths, queries, cache_keys, cache_values, fresh_keys, fresh_values, stream,
        norm_gain.reshape(depth // 128, 128), router.T, routes.T,
        expert_gate, expert_up, expert_down,
    )
    return pl.pallas_call(
        deliver,
        out_shape=[jax.ShapeDtypeStruct(x.shape, x.dtype) for x in results],
        in_specs=[vmem] * 3,
        out_specs=[hbm] * 3,
        scratch_shapes=[dma((3,))],
    )(*results)


def solution(mesh):
    rows = ("groups", "ranks")
    return jax.shard_map(
        functools.partial(shards, mesh.shape["ranks"]),
        mesh=mesh,
        in_specs=(
            P(rows, "tp"), P(rows, None, "tp"), P(rows, None, "tp"), P(rows, "tp"),
            P(rows, "tp"), P(rows, None), P(rows), P(rows, None), P(), P(), P(rows, None),
            P(None, ("ranks", "tp")), P(None, ("ranks", "tp")), P(("ranks", "tp"), None),
        ),
        out_specs=(P(rows, "tp"), P(rows, None, "tp"), P(rows, None, "tp")),
        check_vma=False,
    )
```

```python
import functools

import jax
import jax.numpy as jnp
from jax import lax
from jax.experimental import pallas as pl
from jax.experimental.pallas import tpu as pltpu
from jax.sharding import PartitionSpec as P

HD = 128
EPSILON = 1e-05
F32 = jnp.float32
BF16 = jnp.bfloat16
MESH = pl.DeviceIdType.MESH
SLOTS = 9


def iota(shape, axis):
    return lax.broadcasted_iota(jnp.int32, shape, axis)


def kernel(
    sizes,
    table, lens, q_ref, pk_ref, pv_ref, fk_ref, fv_ref, stream_ref, gain_ref,
    router_ref, routes, gate_hbm, up_hbm, down_hbm,
    out_ref, mk_ref, mv_ref,
    wbuf, kv0, q_s, gain_s, router_s, attn_s, tok_a, tok_b, normed_s, e1_s, e2_s, hid_s,
    sib_s, sib_r, ret_s, ret_r,
    w_sem, d_sem, bar_a_send, bar_a_recv, tok_b_send, tok_b_recv,
    sib_send, sib_recv, ret_send, ret_recv, mv_send, mv_recv,
):
    ranks, experts, requests, ctx, blk, groups, share, depth, hidden, fc, slots = sizes
    half = depth // 2
    quarter = half // 2
    me = lax.axis_index("ranks")
    tp = lax.axis_index("tp")
    other = 1 - tp
    partner = lax.rem(me + ranks // 2, ranks)
    tokens = ranks * requests
    chunks = hidden // fc
    stacked = depth // hidden
    cols = depth // fc
    nj = cols // 2
    nm = nj // 2

    barrier = pltpu.get_barrier_semaphore()

    def greet(d, _):
        pl.semaphore_signal(
            barrier, inc=1, device_id={"ranks": lax.rem(me + d, ranks)}, device_id_type=MESH
        )
        return 0

    lax.fori_loop(1, ranks, greet, 0)
    pl.semaphore_signal(barrier, inc=1, device_id={"tp": other}, device_id_type=MESH)

    def gu_copy(u):
        src = gate_hbm if u % 2 == 0 else up_hbm
        return pltpu.make_async_copy(
            src.at[:, pl.ds((u // 2) * fc, fc)], wbuf.at[u % slots], w_sem.at[u]
        )

    def d_copy(n):
        at = (
            (other * nj + n) if n < nj else (tp * nj + (n - nj))
        )
        u = 2 * chunks + n // stacked
        return pltpu.make_async_copy(
            down_hbm.at[:, pl.ds(pl.multiple_of(at * fc, fc), fc)],
            wbuf.at[u % slots, pl.ds((n % stacked) * hidden, hidden)],
            d_sem.at[n],
        )

    def start_unit(u):
        if u < 2 * chunks:
            gu_copy(u).start()
        else:
            first = (u - 2 * chunks) * stacked
            for n in range(first, min(first + stacked, cols)):
                d_copy(n).start()

    units = 2 * chunks + -(-cols // stacked)
    for u in range(min(slots, units)):
        start_unit(u)
    started = min(slots, units)

    q_s[...] = jnp.zeros_like(q_s)
    for h in range(groups * share):
        q_s[h // share, :, h % share, :] = q_ref[:, h * HD:(h + 1) * HD].astype(F32)
    gains = gain_ref[...].astype(F32)
    for k in range(depth // 128):
        gain_s[:, k * 128:(k + 1) * 128] = gains[k:k + 1]
    router_s[...] = jnp.zeros_like(router_s)
    router_s[:experts] = router_ref[...].astype(F32)

    def attend(i, _):
        limit = lens[i]
        pos = iota((ctx, groups * HD), 0)
        row = iota((requests, groups * HD), 0)

        def logical(pool, fresh):
            x = jnp.concatenate(
                [pool[table[i, j]].astype(F32) for j in range(ctx // blk)], axis=0
            )
            new = jnp.sum(jnp.where(row == i, fresh[...].astype(F32), 0.0), axis=0, keepdims=True)
            return jnp.where(pos < limit, x, jnp.where(pos == limit, new, 0.0)).astype(BF16)

        keys = logical(pk_ref, fk_ref)
        values = logical(pv_ref, fv_ref)

        @pl.when(i == 0)
        def _():
            kv0[0] = keys
            kv0[1] = values

        for g in range(groups):
            q = q_s[g, i].astype(BF16)
            s = lax.dot_general(
                q, keys[:, g * HD:(g + 1) * HD], (((1,), (1,)), ((), ())),
                preferred_element_type=F32,
            ) * HD ** (-0.5)
            s = jnp.where(iota(s.shape, 1) <= limit, s, -1e30)
            p = jnp.exp(s - jnp.max(s, axis=1, keepdims=True))
            p = (p / jnp.sum(p, axis=1, keepdims=True)).astype(BF16)
            o = jnp.dot(p, values[:, g * HD:(g + 1) * HD], preferred_element_type=F32)
            for h in range(share):
                attn_s[g * share + h, pl.ds(i, 1), :] = o[h:h + 1, :]
        return 0

    lax.fori_loop(0, requests, attend, 0, unroll=4)

    own = stream_ref[:, pl.ds(pl.multiple_of(tp * half, half), half)].astype(F32)
    attn = jnp.concatenate([attn_s[h] for h in range(groups * share)], axis=1)
    mid = own + attn.astype(BF16).astype(F32)
    tok_a[me, :, :quarter] = jnp.concatenate(
        [mid[:, :quarter], mid[:, quarter:]], axis=0
    ).astype(BF16)
    which = iota((2 * requests, 128), 0)
    ext = jnp.zeros((2 * requests, 128), F32)
    for t in range(requests):
        for e in range(2):
            ext = jnp.where(which == e * requests + t, routes[e, t].astype(F32), ext)
    tok_a[me, :, quarter:] = ext.astype(BF16)

    pl.semaphore_wait(barrier, ranks)

    def mate_of(r):
        return r + 1 - 2 * lax.rem(r, 2)

    mate = mate_of(me)

    def a_copy(p, src, s):
        return pltpu.make_async_remote_copy(
            src_ref=tok_a.at[src], dst_ref=tok_a.at[src],
            send_sem=bar_a_send.at[s], recv_sem=bar_a_recv.at[src],
            device_id={"ranks": p}, device_id_type=MESH,
        )

    def b_copy(r):
        return pltpu.make_async_remote_copy(
            src_ref=tok_a.at[r], dst_ref=tok_b.at[r],
            send_sem=tok_b_send.at[r], recv_sem=tok_b_recv.at[r],
            device_id={"tp": other}, device_id_type=MESH,
        )

    def send_a(d, _):
        p = lax.rem(me + 2 * d, ranks)
        a_copy(p, me, p).start()
        return 0

    lax.fori_loop(1, ranks // 2, send_a, 0)
    a_copy(mate, me, mate).start()
    b_copy(me).start()
    a_copy(mate, mate, mate).wait_recv()
    b_copy(mate).start()

    def forward(d, _):
        r = lax.rem(me + ranks - 2 * d, ranks)
        a_copy(r, r, r).wait_recv()
        a_copy(mate, r, mate_of(r)).start()
        b_copy(r).start()
        return 0

    lax.fori_loop(1, ranks // 2, forward, 0)

    def forward_mate(d, _):
        r = mate_of(lax.rem(me + ranks - 2 * d, ranks))
        a_copy(r, r, r).wait_recv()
        b_copy(r).start()
        return 0

    lax.fori_loop(1, ranks // 2, forward_mate, 0)

    moved = [
        pltpu.make_async_remote_copy(
            src_ref=kv0.at[n], dst_ref=ref.at[0],
            send_sem=mv_send.at[n], recv_sem=mv_recv.at[n],
            device_id={"ranks": partner}, device_id_type=MESH,
        )
        for n, ref in enumerate((mk_ref, mv_ref))
    ]

    def wait_b(r, _):
        b_copy(r).wait_recv()
        return 0

    lax.fori_loop(0, ranks, wait_b, 0)
    for copy in moved:
        copy.start()

    def served(tok, r):
        swap = lax.rem(iota((2 * requests, quarter), 0), requests) == 0
        far = tok[lax.rem(r + ranks // 2, ranks), :, :quarter].astype(F32)
        x = jnp.where(swap, far, tok[r, :, :quarter].astype(F32))
        return x[:requests], x[requests:]

    at_a = pl.multiple_of(tp * half, half)
    at_b = pl.multiple_of(other * half, half)
    places = (
        at_a, pl.multiple_of(at_a + quarter, quarter),
        at_b, pl.multiple_of(at_b + quarter, quarter),
    )

    def normalise(m, _):
        rows = []
        for r in (2 * m, 2 * m + 1):
            parts = served(tok_a, r) + served(tok_b, r)
            square = sum(jnp.sum(x * x, axis=1, keepdims=True) for x in parts)
            scale = lax.rsqrt(square / depth + EPSILON)
            rows.append([x * scale for x in parts])
            ext = tok_a[r, :, quarter:].astype(F32)
            base = pl.multiple_of(r * requests, requests)
            e1_s[pl.ds(base, requests), :] = ext[:requests]
            e2_s[pl.ds(base, requests), :] = ext[requests:]
        span = pl.ds(pl.multiple_of(m * 2 * requests, 2 * requests), 2 * requests)
        for n, place in enumerate(places):
            x = jnp.concatenate([rows[0][n], rows[1][n]], axis=0)
            gain = gain_s[:, pl.ds(place, quarter)]
            normed_s[span, pl.ds(place, quarter)] = (x * gain).astype(BF16)
        return 0

    lax.fori_loop(0, ranks // 2, normalise, 0, unroll=2)

    logits = lax.dot_general(
        normed_s[...], router_s[...].astype(BF16), (((1,), (1,)), ((), ())), preferred_element_type=F32
    )
    lane = iota(logits.shape, 1).astype(F32)
    e1, e2 = e1_s[:, :1], e2_s[:, :1]
    first = jnp.sum(jnp.where(lane == e1, logits, 0.0), axis=1, keepdims=True)
    second = jnp.sum(jnp.where(lane == e2, logits, 0.0), axis=1, keepdims=True)
    share1 = jax.nn.sigmoid(first - second)
    mine = (me // (ranks // experts)).astype(F32)
    weight = jnp.where(e1 == mine, share1, 0.0) + jnp.where(e2 == mine, 1.0 - share1, 0.0)

    kstep = depth // 3
    for c in range(chunks):
        gu_copy(2 * c).wait()
        gu_copy(2 * c + 1).wait()
        gs, us = (2 * c) % slots, (2 * c + 1) % slots

        def step(k, acc):
            span = pl.ds(pl.multiple_of(k * kstep, kstep), kstep)
            x = normed_s[:, span]
            return (
                acc[0] + jnp.dot(x, wbuf[gs, span, :], preferred_element_type=F32),
                acc[1] + jnp.dot(x, wbuf[us, span, :], preferred_element_type=F32),
            )

        zero = jnp.zeros((tokens, fc), F32)
        g, u = lax.fori_loop(0, 3, step, (zero, zero), unroll=True)
        hid_s[:, c * fc:(c + 1) * fc] = (jax.nn.silu(g) * u).astype(BF16)
        for _ in range(2):
            if started < units:
                start_unit(started)
                started += 1
    assert started == units

    def sib_copy(j):
        return pltpu.make_async_remote_copy(
            src_ref=sib_s.at[j], dst_ref=sib_r.at[j],
            send_sem=sib_send.at[j], recv_sem=sib_recv.at[j],
            device_id={"tp": other}, device_id_type=MESH,
        )

    def ret_copy(m, p, src):
        return pltpu.make_async_remote_copy(
            src_ref=ret_s.at[m, p], dst_ref=ret_r.at[m, src],
            send_sem=ret_send.at[m, p], recv_sem=ret_recv.at[m, src],
            device_id={"ranks": p}, device_id_type=MESH,
        )

    held = None
    for n in range(cols):
        d_copy(n).wait()
        slot = (2 * chunks + n // stacked) % slots
        w = wbuf[slot, (n % stacked) * hidden:(n % stacked + 1) * hidden, :]
        y = jnp.dot(hid_s[...], w, preferred_element_type=F32) * weight
        if n < nj:
            sib_s[n] = y.astype(BF16)
            sib_copy(n).start()
            continue
        j = n - nj
        sib_copy(j).wait_recv()
        y = (y + sib_r[j].astype(F32)).reshape(ranks, requests, fc)
        if j % 2 == 0:
            held = y
            continue
        m = j // 2
        ret_s[m] = jnp.concatenate([held, y], axis=1).astype(BF16)

        def send_ret(d, _, m=m):
            p = lax.rem(me + d, ranks)
            ret_copy(m, p, me).start()
            return 0

        lax.fori_loop(1, ranks, send_ret, 0)

    lo, hi = served(tok_a, me)
    mid_now = jnp.concatenate([lo, hi], axis=1)
    for m in range(nm):
        def gather(d, total, m=m):
            r = lax.rem(me + ranks - d, ranks)
            ret_copy(m, r, r).wait_recv()
            return total + ret_r[m, r].astype(F32)

        total = lax.fori_loop(1, ranks, gather, ret_s[m, me].astype(F32))
        for b in range(2):
            span = slice((2 * m + b) * fc, (2 * m + b + 1) * fc)
            out_ref[:, span] = (
                mid_now[:, span] + total[b * requests:(b + 1) * requests]
            ).astype(BF16)

    def drain(d, _):
        p = lax.rem(me + d, ranks)
        for m in range(nm):
            ret_copy(m, p, me).wait_send()
        return 0

    lax.fori_loop(1, ranks, drain, 0)

    def drain_a(d, _):
        p = lax.rem(me + 2 * d, ranks)
        a_copy(p, me, p).wait_send()
        a_copy(mate, p, mate_of(p)).wait_send()
        return 0

    lax.fori_loop(1, ranks // 2, drain_a, 0)
    a_copy(mate, me, mate).wait_send()

    def drain_b(r, _):
        b_copy(r).wait_send()
        return 0

    lax.fori_loop(0, ranks, drain_b, 0)
    for j in range(nj):
        sib_copy(j).wait_send()
    for copy in moved:
        copy.wait()


def deliver(*refs):
    copies = [pltpu.make_async_copy(refs[n], refs[3 + n], refs[6].at[n]) for n in range(3)]
    for copy in copies:
        copy.start()
    for copy in copies:
        copy.wait()


def shards(
    ranks, queries, cache_keys, cache_values, fresh_keys, fresh_values, block_table, lengths,
    stream, norm_gain, router, routes, expert_gate, expert_up, expert_down,
):
    requests, half = queries.shape
    depth = 2 * half
    experts = router.shape[1]
    blk, width = cache_keys.shape[1:]
    ctx = block_table.shape[1] * blk
    groups = width // HD
    share = half // HD // groups
    hidden = expert_gate.shape[1]
    fc = min(512, hidden)
    chunks = hidden // fc
    cols = depth // fc
    nj = cols // 2
    nm = nj // 2
    quarter = half // 2
    tokens = ranks * requests
    units = 2 * chunks + -(-cols // (depth // hidden))
    slots = min(SLOTS, units)
    sizes = (ranks, experts, requests, ctx, blk, groups, share, depth, hidden, fc, slots)
    vmem = pl.BlockSpec(memory_space=pltpu.VMEM)
    smem = pl.BlockSpec(memory_space=pltpu.SMEM)
    hbm = pl.BlockSpec(memory_space=pl.ANY)
    dma = pltpu.SemaphoreType.DMA
    tok = quarter + 128
    moved = jax.ShapeDtypeStruct((1, ctx, width), BF16)
    results = pl.pallas_call(
        functools.partial(kernel, sizes),
        out_shape=(jax.ShapeDtypeStruct((requests, half), BF16), moved, moved),
        in_specs=[smem, smem] + [vmem] * 8 + [smem] + [hbm] * 3,
        out_specs=(vmem, hbm, hbm),
        scratch_shapes=[
            pltpu.VMEM((slots, depth, fc), BF16),
            pltpu.VMEM((2, ctx, width), BF16),
            pltpu.VMEM((groups, requests, 8 * -(-share // 8), HD), F32),
            pltpu.VMEM((1, depth), F32),
            pltpu.VMEM((8 * -(-experts // 8), depth), F32),
            pltpu.VMEM((half // HD, requests, HD), F32),
            pltpu.VMEM((ranks, 2 * requests, tok), BF16),
            pltpu.VMEM((ranks, 2 * requests, tok), BF16),
            pltpu.VMEM((tokens, depth), BF16),
            pltpu.VMEM((tokens, 128), F32),
            pltpu.VMEM((tokens, 128), F32),
            pltpu.VMEM((tokens, hidden), BF16),
            pltpu.VMEM((nj, tokens, fc), BF16),
            pltpu.VMEM((nj, tokens, fc), BF16),
            pltpu.VMEM((nm, ranks, 2 * requests, fc), BF16),
            pltpu.VMEM((nm, ranks, 2 * requests, fc), BF16),
            dma((2 * chunks,)),
            dma((cols,)),
            dma((ranks,)),
            dma((ranks,)),
            dma((ranks,)),
            dma((ranks,)),
            dma((nj,)),
            dma((nj,)),
            dma((nm, ranks)),
            dma((nm, ranks)),
            dma((2,)),
            dma((2,)),
        ],
        compiler_params=pltpu.CompilerParams(
            collective_id=0, has_side_effects=True, vmem_limit_bytes=62 * 1024 * 1024
        ),
    )(
        block_table, lengths, queries, cache_keys, cache_values, fresh_keys, fresh_values, stream,
        norm_gain.reshape(depth // 128, 128), router.T, routes.T,
        expert_gate, expert_up, expert_down,
    )
    return pl.pallas_call(
        deliver,
        out_shape=[jax.ShapeDtypeStruct(x.shape, x.dtype) for x in results],
        in_specs=[vmem] * 3,
        out_specs=[hbm] * 3,
        scratch_shapes=[dma((3,))],
    )(*results)


def solution(mesh):
    rows = ("groups", "ranks")
    return jax.shard_map(
        functools.partial(shards, mesh.shape["ranks"]),
        mesh=mesh,
        in_specs=(
            P(rows, "tp"), P(rows, None, "tp"), P(rows, None, "tp"), P(rows, "tp"),
            P(rows, "tp"), P(rows, None), P(rows), P(rows, None), P(), P(), P(rows, None),
            P(None, ("ranks", "tp")), P(None, ("ranks", "tp")), P(("ranks", "tp"), None),
        ),
        out_specs=(P(rows, "tp"), P(rows, None, "tp"), P(rows, None, "tp")),
        check_vma=False,
    )
```
